512 devices in a mesh: view: 32 (over y, z_lo, core), row: 16 (over z_hi, x).
Axes of the slice: x: 4, y: 4, z: 16 (z_hi: 4, z_lo: 4; z = z_hi * 4 + z_lo), core: 2. Of those that a mesh axis runs over, the one named last changes fastest.
Arguments:
- queries: bfloat16 [32, 64, 64, 2048], P('view', 'row'), may hold values from -60 to 60
- target_keys: bfloat16 [32, 64, 64, 2048], P('view', 'row'), may hold values from -6 to 6
- target_values: bfloat16 [32, 64, 64, 2048], P('view', 'row'), may hold values from -6 to 6
- cond_keys: bfloat16 [512, 2048], P(('view', 'row')), may hold values from -21 to 21
- cond_values: bfloat16 [512, 2048], P(('view', 'row')), may hold values from -6 to 6
Outputs:
- attended: bfloat16 [32, 64, 64, 2048], P('view', 'row')
The draws below stay inside these ranges and needn't reach their ends.
All inputs are finite; a program needn't handle non-finite values.
Results may differ from the reference program's by a relative error of at most 0.0089.
Values may be sent and summed in bfloat16 or wider, within the bound.
A program may use at most 64 MiB of HBM per device.

```python
import jax
import jax.numpy as jnp
from jax import lax

HEADS = 16
HD = 128
RADIUS = 8
COLS = 64
VIEWS = 32
ROWS = 64
CTOK = 512


def draw_queries(key, part):
    shape = (VIEWS, ROWS, COLS, HEADS, HD)
    drawn = 2.0 * jax.random.truncated_normal(jax.random.fold_in(key, 11), -3.0, 3.0, shape, jnp.float32)
    return drawn.reshape(VIEWS, ROWS, COLS, HEADS * HD).astype(jnp.bfloat16)


def draw_cond_keys(key, part):
    shape = (CTOK, HEADS, HD)
    drawn = jax.random.truncated_normal(jax.random.fold_in(key, 21), -6.0, 6.0, shape, jnp.float32)
    return drawn.reshape(CTOK, HEADS * HD).astype(jnp.bfloat16)


def block_levels(stream_key, shape, split, least, largest):
    def one(position, shards_of):
        draws = jax.random.uniform(jax.random.fold_in(jax.random.fold_in(stream_key, 6), position), (shards_of,), jnp.float32, least / len(split), largest / len(split))
        return jnp.repeat(jnp.exp(draws), shape[position] // shards_of).reshape((-1,) + (1,) * (len(shape) - position - 1))

    gain = one(*split[0])
    for cut in split[1:]:
        gain = gain * one(*cut)
    return gain


def bell_draw(rng, shape, spread, bound, pieces=(), held_as=jnp.bfloat16):
    values = spread * jax.random.normal(rng, shape, jnp.float32)
    if pieces:
        values = values * block_levels(rng, shape, pieces, -0.22, 0.18)
    return jnp.clip(values, -bound, bound).astype(held_as)


def setup_inputs(seed: int = 0) -> dict:
    keys = jax.random.split(jax.random.key(seed), 6)
    queries = draw_queries(jax.random.fold_in(keys[5], 71), 0)
    target_keys = bell_draw(keys[1], (VIEWS, ROWS, COLS, HEADS * HD), 1.0, 6.0, ((0, 32), (1, 16)))
    target_values = bell_draw(keys[2], (VIEWS, ROWS, COLS, HEADS * HD), 1.0, 6.0, ((0, 32), (1, 16)))
    cond_keys = draw_cond_keys(jax.random.fold_in(keys[5], 71), 0)
    cond_values = bell_draw(keys[4], (CTOK, HEADS * HD), 1.0, 6.0, ((0, 512),))
    return dict(queries=queries, target_keys=target_keys, target_values=target_values, cond_keys=cond_keys, cond_values=cond_values)


BASE = 10000.0
NEG_FILL = -1.0e30


def group_layout(head_dim):
    view_width = head_dim // 4
    row_width = 3 * head_dim // 8
    return ((0, view_width), (view_width, row_width), (view_width + row_width, head_dim - view_width - row_width))


def rotary(features, coords):
    outputs = []
    for group_index, (offset, group_width) in enumerate(group_layout(features.shape[-1])):
        half_width = group_width // 2
        lower_part = features[..., offset:offset + half_width]
        upper_part = features[..., offset + half_width:offset + group_width]
        frequency = jnp.power(BASE, -jnp.arange(half_width, dtype=jnp.float32) / half_width)
        angles = coords[..., group_index][..., None, None] * frequency
        cosine = jnp.cos(angles)
        sine = jnp.sin(angles)
        outputs.append(lower_part * cosine - upper_part * sine)
        outputs.append(upper_part * cosine + lower_part * sine)
    return jnp.concatenate(outputs, axis=-1)


def widen(array):
    return lax.optimization_barrier(array).astype(jnp.float32)


def reference(queries, target_keys, target_values, cond_keys, cond_values):
    scale = HD ** -0.5
    span = 2 * RADIUS + 1
    cond_index = jnp.arange(CTOK, dtype=jnp.int32)
    cond_coords = jnp.stack([jnp.zeros((CTOK,), jnp.float32), (cond_index // COLS).astype(jnp.float32), (cond_index % COLS).astype(jnp.float32)], axis=-1)
    cond_rot = widen(rotary(cond_keys.astype(jnp.float32).reshape(CTOK, HEADS, HD), cond_coords).astype(jnp.bfloat16))
    cond_vals = cond_values.astype(jnp.float32).reshape(CTOK, HEADS, HD)
    grid_rows = jnp.broadcast_to(jnp.arange(ROWS, dtype=jnp.int32)[:, None], (ROWS, COLS)).astype(jnp.float32)
    grid_cols = jnp.broadcast_to(jnp.arange(COLS, dtype=jnp.int32)[None, :], (ROWS, COLS)).astype(jnp.float32)
    col_ids = jnp.arange(COLS, dtype=jnp.int32)
    col_ok = jnp.abs(col_ids[:, None] - col_ids[None, :]) <= RADIUS

    def one_view(operands):
        view_queries, view_keys, view_values, view_id = operands
        view_coord = jnp.ones((ROWS, COLS), jnp.float32) * (view_id + 1).astype(jnp.float32)
        coords = jnp.stack([view_coord, grid_rows, grid_cols], axis=-1)
        q_rot = widen(rotary(view_queries.astype(jnp.float32).reshape(ROWS, COLS, HEADS, HD), coords).astype(jnp.bfloat16))
        k_rot = widen(rotary(view_keys.astype(jnp.float32).reshape(ROWS, COLS, HEADS, HD), coords).astype(jnp.bfloat16))
        padding = ((RADIUS, RADIUS), (0, 0), (0, 0), (0, 0))
        keys_pad = jnp.pad(k_rot, padding)
        values_pad = jnp.pad(view_values.astype(jnp.float32).reshape(ROWS, COLS, HEADS, HD), padding)

        def one_row(row_id):
            row_queries = lax.dynamic_index_in_dim(q_rot, row_id, 0, keepdims=False)
            band_keys = lax.dynamic_slice_in_dim(keys_pad, row_id, span, 0).reshape(span * COLS, HEADS, HD)
            band_values = lax.dynamic_slice_in_dim(values_pad, row_id, span, 0).reshape(span * COLS, HEADS, HD)
            band_rows = row_id + jnp.arange(span, dtype=jnp.int32) - RADIUS
            row_ok = (band_rows >= 0) & (band_rows < ROWS)
            allowed = (row_ok[None, :, None] & col_ok[:, None, :]).reshape(COLS, span * COLS)
            win_scores = jnp.einsum("chd,khd->hck", row_queries, band_keys) * scale
            win_scores = jnp.where(allowed[None], win_scores, NEG_FILL)
            cond_scores = jnp.einsum("chd,nhd->hcn", row_queries, cond_rot) * scale
            row_max = jnp.maximum(jnp.max(win_scores, axis=-1), jnp.max(cond_scores, axis=-1))
            win_weights = jnp.exp(win_scores - row_max[..., None])
            cond_weights = jnp.exp(cond_scores - row_max[..., None])
            denominator = jnp.sum(win_weights, axis=-1) + jnp.sum(cond_weights, axis=-1)
            summed = jnp.einsum("hck,khd->hcd", widen(win_weights.astype(jnp.bfloat16)), band_values)
            summed = summed + jnp.einsum("hcn,nhd->hcd", widen(cond_weights.astype(jnp.bfloat16)), cond_vals)
            result = summed / denominator[..., None]
            return result.transpose(1, 0, 2).reshape(COLS, HEADS * HD).astype(jnp.bfloat16)

        return lax.map(one_row, jnp.arange(ROWS, dtype=jnp.int32))

    return lax.map(one_view, (queries, target_keys, target_values, jnp.arange(VIEWS, dtype=jnp.int32)))
```

```python
import functools
import math

import jax
import jax.numpy as jnp
import numpy as np
from jax import lax
from jax.experimental import pallas as pl
from jax.experimental.pallas import tpu as pltpu
from jax.sharding import PartitionSpec as P

HD = 128
RADIUS = 8
BASE = 10000.0
BIG = 1e30
COLS = 64
NX = 4
NZ = 4
NL = 4
NY = 4
RD = 4
HG = 4
LR = RD * NX
BR = LR + 2 * RADIUS
CT = 512
V, K, Q, O = range(4)
F32 = jnp.float32
BF16 = jnp.bfloat16


def trig_tables(views, rows, cols):
    widths = (HD // 4, 3 * HD // 8, 3 * HD // 8)
    counts = (views + 8, rows, cols)
    tables, offset = [], 0
    for width, count in zip(widths, counts):
        half = width // 2
        freq = np.power(np.float32(BASE), -np.arange(half, dtype=np.float32) / np.float32(half)).astype(np.float32)
        angle = (np.arange(count, dtype=np.float32)[:, None] * freq).astype(np.float64)
        table = np.zeros((2, count, HD), np.float32)
        for i, f in enumerate((np.cos, np.sin)):
            table[i, :, offset : offset + half] = f(angle)
            table[i, :, offset + half : offset + width] = f(angle)
        tables.append(table)
        offset += width
    return tables


def swap_matrix():
    swap, offset = np.zeros((HD, HD), np.float32), 0
    for width in (HD // 4, 3 * HD // 8, 3 * HD // 8):
        half = width // 2
        for i in range(offset, offset + half):
            swap[i + half, i] = -1.0
            swap[i, i + half] = 1.0
        offset += width
    return swap


def kernel(
    q_hbm, k_hbm, v_hbm, ck_ref, cv_ref, vt, rt, ct, swap, out_hbm,
    kin, qin, kst, qst, k_buf, v_buf, q_buf, o_buf, qaug, kaug, cs, cst, c1, ckv,
    lsem, xs, xr, zs, zr, c1s, c1r, ls, lr, ys, yr, ks, kr,
):
    row = lax.axis_index("row")
    view = lax.axis_index("view")
    x, zh = row % NX, row // NX
    core, zl, y = view % 2, (view // 2) % NL, view // (2 * NL)

    def row_dev(zz, xx):
        return {"view": view, "row": zz * NX + xx}

    def view_dev(yy, ll, cc):
        return {"view": (yy * NL + ll) * 2 + cc, "row": row}

    def remote(src, dst, s, r, dev):
        return pltpu.make_async_remote_copy(
            src_ref=src, dst_ref=dst, send_sem=s, recv_sem=r, device_id=dev, device_id_type=pl.DeviceIdType.MESH
        )

    load_k = pltpu.make_async_copy(k_hbm.at[0], kin, lsem.at[0])
    load_q = pltpu.make_async_copy(q_hbm.at[0], qin, lsem.at[1])
    load_k.start()
    load_q.start()

    barrier = pltpu.get_barrier_semaphore()

    def greet(dev):
        pl.semaphore_signal(barrier, inc=1, device_id=dev, device_id_type=pl.DeviceIdType.MESH)

    @pl.loop(1, NX * NZ)
    def _(d):
        greet({"view": view, "row": (row + d) % (NX * NZ)})

    for d in range(1, NL):
        greet(view_dev(y, (zl + d) % NL, core))
    for d in range(1, NY):
        greet(view_dev((y + d) % NY, zl, core))
    greet(view_dev(y, zl, 1 - core))

    for edge, first in ((0, 0), (NZ - 1, RADIUS + LR)):

        @pl.when(zh == edge)
        def _():
            @pl.loop(0, HG)
            def _(h):
                @pl.loop(0, RADIUS)
                def _(r):
                    k_buf[h, first + r] = jnp.zeros((COLS, HD), BF16)
                    v_buf[h, first + r] = jnp.zeros((COLS, HD), BF16)

    for i in range(2):
        base = ct[i] + vt[i, pl.ds(view + 1, 1), :]
        for r in range(RD):
            cs[i, pl.ds(r * COLS, COLS), :] = base + rt[i, pl.ds(row * RD + r, 1), :]

    for h in range(HG * NX):
        p, hh = h // HG, h % HG
        cst[pl.ds(p * 8 + hh, 1), :] = ck_ref[:, pl.ds(h * HD, HD)].astype(F32)
        cst[pl.ds(p * 8 + HG + hh, 1), :] = cv_ref[:, pl.ds(h * HD, HD)].astype(F32)
    token = view * (NX * NZ) + row
    ctok = [vt[i, pl.ds(0, 1), :] + rt[i, pl.ds(token // COLS, 1), :] + ct[i, pl.ds(token % COLS, 1), :] for i in range(2)]
    ckin = cst[...]
    crot = jnp.dot(ckin.astype(BF16), swap[...], preferred_element_type=F32)
    crot = (ckin * ctok[0] + crot * ctok[1]).astype(BF16).astype(F32)
    is_key = lax.broadcasted_iota(jnp.int32, (8 * NX, HD), 0) % 8 < HG
    cst[...] = jnp.where(is_key, crot, ckin)
    c1[pl.ds(pl.multiple_of(row * 8, 8), 8), :] = cst[pl.ds(pl.multiple_of(x * 8, 8), 8), :]

    pl.semaphore_wait(barrier, NX * NZ - 1 + NL - 1 + NY - 1 + 1)

    def own_rows(buf, h, xx):
        return buf.at[h, pl.ds(RADIUS + RD * xx, RD)]

    def x_src(kind, h, p):
        if kind == V:
            return v_hbm.at[0, :, :, pl.ds(pl.multiple_of((HG * p + h) * HD, HD), HD)]
        return (kst if kind == K else qst).at[p, h]

    def x_dst(kind, h, xx):
        if kind == Q:
            return q_buf.at[h, pl.ds(RD * xx, RD)]
        return own_rows(k_buf if kind == K else v_buf, h, xx)

    def x_copy(kind, h, d):
        p = (x + d) % NX
        return remote(x_src(kind, h, p), x_dst(kind, h, x), xs.at[kind, h, p], xr.at[kind, h, x], row_dev(zh, p))

    def x_own(kind, h):
        return pltpu.make_async_copy(x_src(kind, h, x), x_dst(kind, h, x), xs.at[kind, h, x])

    def x_send(kind, h):
        for d in (2, 1, 3):
            x_copy(kind, h, d).start()
        x_own(kind, h).start()

    def x_wait(kind, h):
        for d in (1, 2, 3):
            p = (x + d) % NX
            remote(x_src(kind, h, x), x_dst(kind, h, p), xs.at[kind, h, x], xr.at[kind, h, p], row_dev(zh, p)).wait_recv()
        x_own(kind, h).wait()

    def rope(src, dst, h):
        @pl.loop(0, NX)
        def _(p):
            feats = src[:, :, pl.ds(pl.multiple_of((HG * p + h) * HD, HD), HD)].reshape(RD * COLS, HD)
            turned = jnp.dot(feats, swap[...], preferred_element_type=F32)
            out = feats.astype(F32) * cs[0] + turned * cs[1]
            dst[p, h] = out.astype(BF16).reshape(RD, COLS, HD)

    def z_copy(kind, h, up):
        buf = k_buf if kind == K else v_buf
        src = buf.at[h, pl.ds(LR if up else RADIUS, RADIUS)]
        dst = buf.at[h, pl.ds(0 if up else RADIUS + LR, RADIUS)]
        return remote(src, dst, zs.at[up, kind, h], zr.at[up, kind, h], row_dev(zh + (1 if up else -1), x))

    def z_both(kind, h, act_up, act_down):
        pl.when(zh < NZ - 1)(lambda: act_up(z_copy(kind, h, 1)))
        pl.when(zh > 0)(lambda: act_down(z_copy(kind, h, 0)))

    def forward(kind, h):
        x_wait(kind, h)
        z_both(kind, h, lambda c: c.start(), lambda c: c.start())

    def c1_copy(d):
        peer = (row + d) % (NX * NZ)
        return remote(
            cst.at[pl.ds(pl.multiple_of((peer % NX) * 8, 8), 8), :],
            c1.at[pl.ds(pl.multiple_of(row * 8, 8), 8), :],
            c1s.at[peer], c1r.at[row], {"view": view, "row": peer},
        )

    def c1_wait(d):
        peer = (row + d) % (NX * NZ)
        remote(
            cst.at[pl.ds(0, 8), :],
            c1.at[pl.ds(pl.multiple_of(peer * 8, 8), 8), :],
            c1s.at[peer], c1r.at[peer], {"view": view, "row": peer},
        ).wait_recv()

    def slot(yy, ll, cc, blocks):
        return ckv.at[:, pl.ds(pl.multiple_of(((cc * NY + yy) * NL + ll) * 16, 16), blocks * 16), :]

    def l_copy(d):
        peer = (zl + d) % NL
        return remote(slot(y, zl, core, 1), slot(y, zl, core, 1), ls.at[peer], lr.at[zl], view_dev(y, peer, core))

    def l_wait(d):
        peer = (zl + d) % NL
        remote(slot(y, zl, core, 1), slot(y, peer, core, 1), ls.at[peer], lr.at[peer], view_dev(y, peer, core)).wait_recv()

    def y_copy(d):
        peer = (y + d) % NY
        return remote(slot(y, 0, core, NL), slot(y, 0, core, NL), ys.at[peer], yr.at[y], view_dev(peer, zl, core))

    def y_wait(d):
        peer = (y + d) % NY
        remote(slot(y, 0, core, NL), slot(peer, 0, core, NL), ys.at[peer], yr.at[peer], view_dev(peer, zl, core)).wait_recv()

    def core_copy(cc):
        return remote(slot(0, 0, cc, NL * NY), slot(0, 0, cc, NL * NY), ks.at[0], kr.at[0], view_dev(y, zl, 1 - core))

    x_send(V, 0)
    pl.loop(1, NX * NZ)(lambda d: c1_copy(d).start())
    load_k.wait()
    for h in range(HG):
        if h:
            x_send(V, h)
        rope(kin, kst, h)
        x_send(K, h)

    @pl.loop(0, LR)
    def _(r):
        lane = lax.broadcasted_iota(jnp.int32, (COLS, HD), 1)
        col = lax.broadcasted_iota(jnp.int32, (COLS, HD), 0)
        low = jnp.where(zh == 0, 80, -1)
        high = jnp.where(zh == NZ - 1, 81, -1)
        on = (lane == col) | (lane == r + COLS) | (lane == low) | (lane == high)
        qaug[r] = jnp.where(on, 1.0, 0.0).astype(BF16)

    @pl.loop(0, BR)
    def _(r):
        lane = lax.broadcasted_iota(jnp.int32, (COLS, HD), 1)
        col = lax.broadcasted_iota(jnp.int32, (COLS, HD), 0)
        low = jnp.where(r < RADIUS, 80, -1)
        high = jnp.where(r >= RADIUS + LR, 81, -1)
        far_col = (lane < COLS) & (jnp.abs(lane - col) > RADIUS)
        apart = r - (lane - COLS)
        far_row = (lane >= COLS) & (lane < COLS + LR) & ((apart < 0) | (apart > 2 * RADIUS))
        off = far_col | far_row | (lane == low) | (lane == high)
        kaug[r] = jnp.where(off, -BIG, 0.0).astype(BF16)

    forward(V, 0)
    forward(K, 0)
    pl.loop(1, NX * NZ)(c1_wait)
    for i in range(8):
        rows16 = c1[pl.ds(i, NX * NZ, stride=8), :]
        ckv[i, pl.ds(pl.multiple_of(((core * NY + y) * NL + zl) * 16, 16), 16), :] = rows16.astype(BF16)
    for d in range(1, NL):
        l_copy(d).start()
    load_q.wait()
    for h in range(HG):
        rope(qin, qst, h)
        x_send(Q, h)
    forward(V, 1)
    forward(K, 1)
    for d in range(1, NL):
        l_wait(d)
    for d in range(1, NY):
        y_copy(d).start()
    forward(V, 2)
    forward(K, 2)
    for d in range(1, NY):
        y_wait(d)
    core_copy(core).start()
    forward(V, 3)
    forward(K, 3)
    core_copy(1 - core).wait_recv()

    def o_copy(h, b):
        return remote(
            o_buf.at[h, pl.ds(RD * b, RD)],
            out_hbm.at[0, :, :, pl.ds(pl.multiple_of((HG * x + h) * HD, HD), HD)],
            xs.at[O, h, b], xr.at[O, h, x], row_dev(zh, b),
        )

    def o_own(h):
        return pltpu.make_async_copy(
            o_buf.at[h, pl.ds(RD * x, RD)],
            out_hbm.at[0, :, :, pl.ds(pl.multiple_of((HG * x + h) * HD, HD), HD)],
            xs.at[O, h, x],
        )

    def o_wait(h, p):
        remote(
            o_buf.at[h, pl.ds(RD * p, RD)],
            out_hbm.at[0, :, :, pl.ds(pl.multiple_of((HG * p + h) * HD, HD), HD)],
            xs.at[O, h, p], xr.at[O, h, p], row_dev(zh, p),
        ).wait_recv()

    scale = math.log2(math.e) / math.sqrt(HD)
    nt = (((1,), (1,)), ((), ()))

    def block(h, b):
        n, band = RD * COLS, (RD + 2 * RADIUS) * COLS
        qb = q_buf[h, pl.ds(RD * b, RD)].reshape(n, HD)
        qa = qaug[pl.ds(RD * b, RD)].reshape(n, HD)
        kb = k_buf[h, pl.ds(RD * b, RD + 2 * RADIUS)].reshape(band, HD)
        ka = kaug[pl.ds(RD * b, RD + 2 * RADIUS)].reshape(band, HD)
        s1 = lax.dot_general(
            jnp.concatenate([qb, qa], axis=1), jnp.concatenate([kb, ka], axis=1), nt, preferred_element_type=F32
        )
        s2 = lax.dot_general(qb, ckv[h], nt, preferred_element_type=F32)
        m = jnp.maximum(jnp.max(s1, axis=1, keepdims=True), jnp.max(s2, axis=1, keepdims=True))
        p1 = jnp.exp2((s1 - m) * scale).astype(BF16)
        p2 = jnp.exp2((s2 - m) * scale).astype(BF16)
        vb = v_buf[h, pl.ds(RD * b, RD + 2 * RADIUS)].reshape(band, HD)
        acc = jnp.dot(p1, jnp.concatenate([vb, jnp.ones((band, HD), BF16)], axis=1), preferred_element_type=F32)
        acc += jnp.dot(
            p2, jnp.concatenate([ckv[HG + h], jnp.ones((CT, HD), BF16)], axis=1), preferred_element_type=F32
        )
        o_buf[h, pl.ds(RD * b, RD)] = (acc[:, :HD] / acc[:, HD:]).astype(BF16).reshape(RD, COLS, HD)

    @pl.loop(0, HG)
    def _(h):
        x_wait(Q, h)
        for kind in (V, K):
            pl.when(zh > 0)(lambda: z_copy(kind, h, 1).wait_recv())
            pl.when(zh < NZ - 1)(lambda: z_copy(kind, h, 0).wait_recv())

        @pl.loop(1, NX)
        def _(d):
            b = (x + d) % NX
            block(h, b)
            o_copy(h, b).start()

        block(h, x)
        o_own(h).start()

    @pl.loop(0, HG)
    def _(h):
        for d in range(1, NX):
            p = (x + d) % NX
            o_wait(h, p)
            o_copy(h, p).wait_send()
            for kind in (V, K, Q):
                x_copy(kind, h, d).wait_send()
        o_own(h).wait()
        for kind in (V, K):
            z_both(kind, h, lambda c: c.wait_send(), lambda c: c.wait_send())

    pl.loop(1, NX * NZ)(lambda d: c1_copy(d).wait_send())
    for d in range(1, NL):
        l_copy(d).wait_send()
    for d in range(1, NY):
        y_copy(d).wait_send()
    core_copy(core).wait_send()


def local(queries, target_keys, target_values, cond_keys, cond_values):
    rows = queries.shape[1] * NX * NZ
    views = 2 * NL * NY
    vt, rt, ct = trig_tables(views, rows, COLS)
    vmem, hbm = pl.BlockSpec(memory_space=pltpu.VMEM), pl.BlockSpec(memory_space=pl.ANY)
    heads = HG * NX
    dma = pltpu.SemaphoreType.DMA
    return pl.pallas_call(
        kernel,
        out_shape=jax.ShapeDtypeStruct(queries.shape, BF16),
        in_specs=[hbm] * 3 + [vmem] * 6,
        out_specs=hbm,
        scratch_shapes=[
            pltpu.VMEM((RD, COLS, heads * HD), BF16),
            pltpu.VMEM((RD, COLS, heads * HD), BF16),
            pltpu.VMEM((NX, HG, RD, COLS, HD), BF16),
            pltpu.VMEM((NX, HG, RD, COLS, HD), BF16),
            pltpu.VMEM((HG, BR, COLS, HD), BF16),
            pltpu.VMEM((HG, BR, COLS, HD), BF16),
            pltpu.VMEM((HG, LR, COLS, HD), BF16),
            pltpu.VMEM((HG, LR, COLS, HD), BF16),
            pltpu.VMEM((LR, COLS, HD), BF16),
            pltpu.VMEM((BR, COLS, HD), BF16),
            pltpu.VMEM((2, RD * COLS, HD), F32),
            pltpu.VMEM((8 * NX, HD), F32),
            pltpu.VMEM((8 * NX * NZ, HD), F32),
            pltpu.VMEM((2 * HG, CT, HD), BF16),
            dma((2,)),
            dma((4, HG, NX)),
            dma((4, HG, NX)),
            dma((2, 2, HG)),
            dma((2, 2, HG)),
            dma((NX * NZ,)),
            dma((NX * NZ,)),
            dma((NL,)),
            dma((NL,)),
            dma((NY,)),
            dma((NY,)),
            dma((1,)),
            dma((1,)),
        ],
        compiler_params=pltpu.CompilerParams(
            collective_id=0, has_side_effects=True, vmem_limit_bytes=48 * 1024 * 1024
        ),
        cost_estimate=pl.CostEstimate(flops=8_000_000_000, bytes_accessed=5_000_000, transcendentals=8_000_000),
    )(
        queries, target_keys, target_values, cond_keys, cond_values,
        jnp.asarray(vt), jnp.asarray(rt), jnp.asarray(ct), jnp.asarray(swap_matrix(), BF16),
    )


def solution(mesh):
    return jax.shard_map(
        local,
        mesh=mesh,
        in_specs=(
            P("view", "row", None, None),
            P("view", "row", None, None),
            P("view", "row", None, None),
            P(("view", "row"), None),
            P(("view", "row"), None),
        ),
        out_specs=P("view", "row", None, None),
        check_vma=False,
    )
```

```python
import functools
import math

import jax
import jax.numpy as jnp
import numpy as np
from jax import lax
from jax.experimental import pallas as pl
from jax.experimental.pallas import tpu as pltpu
from jax.sharding import PartitionSpec as P

HD = 128
RADIUS = 8
BASE = 10000.0
BIG = 1e30
COLS = 64
NX = 4
NZ = 4
NL = 4
NY = 4
RD = 4
HG = 4
LR = RD * NX
BR = LR + 2 * RADIUS
CT = 512
ROWS = LR * NZ
VIEW_ROWS = 40
VIEW_TAB, ROW_TAB, COL_TAB, SWAP_TAB = 0, 2 * VIEW_ROWS, 2 * (VIEW_ROWS + ROWS), 2 * (VIEW_ROWS + ROWS + COLS)
V, K, Q, O = range(4)
F32 = jnp.float32
BF16 = jnp.bfloat16


def trig_tables(rows, cols):
    widths = (HD // 4, 3 * HD // 8, 3 * HD // 8)
    counts = (VIEW_ROWS, rows, cols)
    tables, offset = [], 0
    for width, count in zip(widths, counts):
        half = width // 2
        freq = np.power(np.float32(BASE), -np.arange(half, dtype=np.float32) / np.float32(half)).astype(np.float32)
        angle = (np.arange(count, dtype=np.float32)[:, None] * freq).astype(np.float64)
        table = np.zeros((2, count, HD), np.float32)
        for i, f in enumerate((np.cos, np.sin)):
            table[i, :, offset : offset + half] = f(angle)
            table[i, :, offset + half : offset + width] = f(angle)
        tables.append(table)
        offset += width
    return tables


def swap_matrix():
    swap, offset = np.zeros((HD, HD), np.float32), 0
    for width in (HD // 4, 3 * HD // 8, 3 * HD // 8):
        half = width // 2
        for i in range(offset, offset + half):
            swap[i + half, i] = -1.0
            swap[i, i + half] = 1.0
        offset += width
    return swap


def kernel(
    q_hbm, k_hbm, v_hbm, ck_hbm, cv_hbm, tab_hbm, out_hbm,
    tab, swap, ck_ref, cv_ref, kin, qin, kst, qst, k_buf, v_buf, q_buf, o_buf, qaug, kaug, cs, cst, c1, ckv,
    lsem, xs, xr, zs, zr, c1s, c1r, ls, lr, ys, yr, ks, kr,
):
    row = lax.axis_index("row")
    view = lax.axis_index("view")
    x, zh = row % NX, row // NX
    core, zl, y = view % 2, (view // 2) % NL, view // (2 * NL)

    def row_dev(zz, xx):
        return {"view": view, "row": zz * NX + xx}

    def view_dev(yy, ll, cc):
        return {"view": (yy * NL + ll) * 2 + cc, "row": row}

    def remote(src, dst, s, r, dev):
        return pltpu.make_async_remote_copy(
            src_ref=src, dst_ref=dst, send_sem=s, recv_sem=r, device_id=dev, device_id_type=pl.DeviceIdType.MESH
        )

    barrier = pltpu.get_barrier_semaphore()

    def greet(dev):
        pl.semaphore_signal(barrier, inc=1, device_id=dev, device_id_type=pl.DeviceIdType.MESH)

    @pl.loop(1, NX * NZ)
    def _(d):
        greet({"view": view, "row": (row + d) % (NX * NZ)})

    for d in range(1, NL):
        greet(view_dev(y, (zl + d) % NL, core))
    for d in range(1, NY):
        greet(view_dev((y + d) % NY, zl, core))
    greet(view_dev(y, zl, 1 - core))

    loads = [
        pltpu.make_async_copy(src, dst, lsem.at[i])
        for i, (src, dst) in enumerate(
            ((tab_hbm, tab), (ck_hbm, ck_ref), (cv_hbm, cv_ref), (k_hbm.at[0], kin), (q_hbm.at[0], qin))
        )
    ]
    for load in loads:
        load.start()

    pl.semaphore_wait(barrier, NX * NZ - 1 + NL - 1 + NY - 1 + 1)

    def own_rows(buf, h, xx):
        return buf.at[h, pl.ds(RADIUS + RD * xx, RD)]

    def x_src(kind, h, p):
        if kind == V:
            return v_hbm.at[0, :, :, pl.ds(pl.multiple_of((HG * p + h) * HD, HD), HD)]
        return (kst if kind == K else qst).at[p, h]

    def x_dst(kind, h, xx):
        if kind == Q:
            return q_buf.at[h, pl.ds(RD * xx, RD)]
        return own_rows(k_buf if kind == K else v_buf, h, xx)

    def x_copy(kind, h, d):
        p = (x + d) % NX
        return remote(x_src(kind, h, p), x_dst(kind, h, x), xs.at[kind, h, p], xr.at[kind, h, x], row_dev(zh, p))

    def x_own(kind, h):
        return pltpu.make_async_copy(x_src(kind, h, x), x_dst(kind, h, x), xs.at[kind, h, x])

    def x_send(kind, h):
        for d in (2, 1, 3):
            x_copy(kind, h, d).start()
        x_own(kind, h).start()

    def x_from(kind, h, p):
        @pl.when(p != x)
        def _():
            remote(x_src(kind, h, x), x_dst(kind, h, p), xs.at[kind, h, x], xr.at[kind, h, p], row_dev(zh, p)).wait_recv()

        @pl.when(p == x)
        def _():
            x_own(kind, h).wait()

    def rope(src, dst, h):
        @pl.loop(0, NX)
        def _(p):
            feats = src[:, :, pl.ds(pl.multiple_of((HG * p + h) * HD, HD), HD)].reshape(RD * COLS, HD)
            turned = jnp.dot(feats, swap[...], preferred_element_type=F32)
            out = feats.astype(F32) * cs[0] + turned * cs[1]
            dst[p, h] = out.astype(BF16).reshape(RD, COLS, HD)

    def z_copy(kind, h, up, far):
        buf = k_buf if kind == K else v_buf
        if up:
            src, dst = RADIUS + LR - RD * (1 + far), RD * (1 - far)
        else:
            src, dst = RADIUS + RD * far, RADIUS + LR + RD * far
        i = 2 * up + far
        return remote(
            buf.at[h, pl.ds(src, RD)], buf.at[h, pl.ds(dst, RD)],
            zs.at[i, kind, h], zr.at[i, kind, h], row_dev(zh + (1 if up else -1), x),
        )

    has_up, has_down = zh < NZ - 1, zh > 0

    def forward(kind, h):
        for far in (0, 1):
            x_from(kind, h, NX - 1 - far)
            pl.when(has_up)(lambda: z_copy(kind, h, 1, far).start())
            x_from(kind, h, far)
            pl.when(has_down)(lambda: z_copy(kind, h, 0, far).start())

    def c1_copy(d):
        peer = (row + d) % (NX * NZ)
        return remote(
            cst.at[pl.ds(pl.multiple_of((peer % NX) * 8, 8), 8), :],
            c1.at[pl.ds(pl.multiple_of(row * 8, 8), 8), :],
            c1s.at[peer], c1r.at[row], {"view": view, "row": peer},
        )

    def c1_wait(d):
        peer = (row + d) % (NX * NZ)
        remote(
            cst.at[pl.ds(0, 8), :],
            c1.at[pl.ds(pl.multiple_of(peer * 8, 8), 8), :],
            c1s.at[peer], c1r.at[peer], {"view": view, "row": peer},
        ).wait_recv()

    def slot(yy, ll, cc, blocks):
        return ckv.at[:, pl.ds(pl.multiple_of(((cc * NY + yy) * NL + ll) * 16, 16), blocks * 16), :]

    def l_copy(d):
        peer = (zl + d) % NL
        return remote(slot(y, zl, core, 1), slot(y, zl, core, 1), ls.at[peer], lr.at[zl], view_dev(y, peer, core))

    def l_wait(d):
        peer = (zl + d) % NL
        remote(slot(y, zl, core, 1), slot(y, peer, core, 1), ls.at[peer], lr.at[peer], view_dev(y, peer, core)).wait_recv()

    def y_copy(d):
        peer = (y + d) % NY
        return remote(slot(y, 0, core, NL), slot(y, 0, core, NL), ys.at[peer], yr.at[y], view_dev(peer, zl, core))

    def y_wait(d):
        peer = (y + d) % NY
        remote(slot(y, 0, core, NL), slot(peer, 0, core, NL), ys.at[peer], yr.at[peer], view_dev(peer, zl, core)).wait_recv()

    def core_copy(cc):
        return remote(slot(0, 0, cc, NL * NY), slot(0, 0, cc, NL * NY), ks.at[0], kr.at[0], view_dev(y, zl, 1 - core))

    x_send(V, 0)
    for load in loads[:3]:
        load.wait()
    swap[...] = tab[pl.ds(SWAP_TAB, HD), :].astype(BF16)

    for i in range(2):
        base = tab[pl.ds(COL_TAB + i * COLS, COLS), :] + tab[pl.ds(VIEW_TAB + i * VIEW_ROWS + view + 1, 1), :]
        for r in range(RD):
            cs[i, pl.ds(r * COLS, COLS), :] = base + tab[pl.ds(ROW_TAB + i * ROWS + row * RD + r, 1), :]

    for h in range(HG * NX):
        p, hh = h // HG, h % HG
        cst[pl.ds(p * 8 + hh, 1), :] = ck_ref[:, pl.ds(h * HD, HD)].astype(F32)
        cst[pl.ds(p * 8 + HG + hh, 1), :] = cv_ref[:, pl.ds(h * HD, HD)].astype(F32)
    token = view * (NX * NZ) + row
    ctok = [
        tab[pl.ds(VIEW_TAB + i * VIEW_ROWS, 1), :]
        + tab[pl.ds(ROW_TAB + i * ROWS + token // COLS, 1), :]
        + tab[pl.ds(COL_TAB + i * COLS + token % COLS, 1), :]
        for i in range(2)
    ]
    ckin = cst[...]
    crot = jnp.dot(ckin.astype(BF16), swap[...], preferred_element_type=F32)
    crot = (ckin * ctok[0] + crot * ctok[1]).astype(BF16).astype(F32)
    is_key = lax.broadcasted_iota(jnp.int32, (8 * NX, HD), 0) % 8 < HG
    cst[...] = jnp.where(is_key, crot, ckin)
    c1[pl.ds(pl.multiple_of(row * 8, 8), 8), :] = cst[pl.ds(pl.multiple_of(x * 8, 8), 8), :]

    pl.loop(1, NX * NZ)(lambda d: c1_copy(d).start())
    for edge, first in ((0, 0), (NZ - 1, RADIUS + LR)):

        @pl.when(zh == edge)
        def _():
            @pl.loop(0, HG)
            def _(h):
                @pl.loop(0, RADIUS)
                def _(r):
                    k_buf[h, first + r] = jnp.zeros((COLS, HD), BF16)
                    v_buf[h, first + r] = jnp.zeros((COLS, HD), BF16)

    loads[3].wait()
    rope(kin, kst, 0)
    x_send(K, 0)
    x_send(V, 1)
    forward(V, 0)
    rope(kin, kst, 1)
    x_send(K, 1)
    forward(K, 0)
    pl.loop(1, NX * NZ)(c1_wait)
    for i in range(8):
        rows16 = c1[pl.ds(i, NX * NZ, stride=8), :]
        ckv[i, pl.ds(pl.multiple_of(((core * NY + y) * NL + zl) * 16, 16), 16), :] = rows16.astype(BF16)
    for d in range(1, NL):
        l_copy(d).start()
    x_send(V, 2)
    rope(kin, kst, 2)
    x_send(K, 2)
    forward(V, 1)
    forward(K, 1)
    x_send(V, 3)
    rope(kin, kst, 3)
    x_send(K, 3)
    forward(V, 2)
    loads[4].wait()
    for h in range(HG):
        rope(qin, qst, h)
        x_send(Q, h)
    forward(K, 2)
    forward(V, 3)
    forward(K, 3)

    @pl.loop(0, LR)
    def _(r):
        lane = lax.broadcasted_iota(jnp.int32, (COLS, HD), 1)
        col = lax.broadcasted_iota(jnp.int32, (COLS, HD), 0)
        low = jnp.where(zh == 0, 80, -1)
        high = jnp.where(zh == NZ - 1, 81, -1)
        on = (lane == col) | (lane == r + COLS) | (lane == low) | (lane == high)
        qaug[r] = jnp.where(on, 1.0, 0.0).astype(BF16)

    @pl.loop(0, BR)
    def _(r):
        lane = lax.broadcasted_iota(jnp.int32, (COLS, HD), 1)
        col = lax.broadcasted_iota(jnp.int32, (COLS, HD), 0)
        low = jnp.where(r < RADIUS, 80, -1)
        high = jnp.where(r >= RADIUS + LR, 81, -1)
        far_col = (lane < COLS) & (jnp.abs(lane - col) > RADIUS)
        apart = r - (lane - COLS)
        far_row = (lane >= COLS) & (lane < COLS + LR) & ((apart < 0) | (apart > 2 * RADIUS))
        off = far_col | far_row | (lane == low) | (lane == high)
        kaug[r] = jnp.where(off, -BIG, 0.0).astype(BF16)

    for d in range(1, NL):
        l_wait(d)
    for d in range(1, NY):
        y_copy(d).start()
    for d in range(1, NY):
        y_wait(d)
    core_copy(core).start()
    core_copy(1 - core).wait_recv()

    def o_copy(h, b):
        return remote(
            o_buf.at[h, pl.ds(RD * b, RD)],
            out_hbm.at[0, :, :, pl.ds(pl.multiple_of((HG * x + h) * HD, HD), HD)],
            xs.at[O, h, b], xr.at[O, h, x], row_dev(zh, b),
        )

    def o_own(h):
        return pltpu.make_async_copy(
            o_buf.at[h, pl.ds(RD * x, RD)],
            out_hbm.at[0, :, :, pl.ds(pl.multiple_of((HG * x + h) * HD, HD), HD)],
            xs.at[O, h, x],
        )

    def o_wait(h, p):
        remote(
            o_buf.at[h, pl.ds(RD * p, RD)],
            out_hbm.at[0, :, :, pl.ds(pl.multiple_of((HG * p + h) * HD, HD), HD)],
            xs.at[O, h, p], xr.at[O, h, p], row_dev(zh, p),
        ).wait_recv()

    scale = math.log2(math.e) / math.sqrt(HD)
    nt = (((1,), (1,)), ((), ()))

    def block(h, b):
        n, band = RD * COLS, (RD + 2 * RADIUS) * COLS
        qb = q_buf[h, pl.ds(RD * b, RD)].reshape(n, HD)
        qa = qaug[pl.ds(RD * b, RD)].reshape(n, HD)
        kb = k_buf[h, pl.ds(RD * b, RD + 2 * RADIUS)].reshape(band, HD)
        ka = kaug[pl.ds(RD * b, RD + 2 * RADIUS)].reshape(band, HD)
        s1 = lax.dot_general(
            jnp.concatenate([qb, qa], axis=1), jnp.concatenate([kb, ka], axis=1), nt, preferred_element_type=F32
        )
        s2 = lax.dot_general(qb, ckv[h], nt, preferred_element_type=F32)
        m = jnp.maximum(jnp.max(s1, axis=1, keepdims=True), jnp.max(s2, axis=1, keepdims=True))
        p1 = jnp.exp2((s1 - m) * scale).astype(BF16)
        p2 = jnp.exp2((s2 - m) * scale).astype(BF16)
        vb = v_buf[h, pl.ds(RD * b, RD + 2 * RADIUS)].reshape(band, HD)
        acc = jnp.dot(p1, jnp.concatenate([vb, jnp.ones((band, HD), BF16)], axis=1), preferred_element_type=F32)
        acc += jnp.dot(
            p2, jnp.concatenate([ckv[HG + h], jnp.ones((CT, HD), BF16)], axis=1), preferred_element_type=F32
        )
        o_buf[h, pl.ds(RD * b, RD)] = (acc[:, :HD] / acc[:, HD:]).astype(BF16).reshape(RD, COLS, HD)

    @pl.loop(0, HG)
    def _(h):
        for p in range(NX):
            x_from(Q, h, p)
        for b in (1, 2, 0, 3):
            up, far = b < NX // 2, b in (0, NX - 1)
            for kind in (V, K):
                pl.when(has_down if up else has_up)(lambda: z_copy(kind, h, up, far).wait_recv())
            block(h, b)
            pl.when(x != b)(lambda: o_copy(h, b).start())
            pl.when(x == b)(lambda: o_own(h).start())

    @pl.loop(0, HG)
    def _(h):
        for d in range(1, NX):
            p = (x + d) % NX
            o_wait(h, p)
            o_copy(h, p).wait_send()
            for kind in (V, K, Q):
                x_copy(kind, h, d).wait_send()
        o_own(h).wait()
        for kind in (V, K):
            for far in (0, 1):
                pl.when(has_up)(lambda: z_copy(kind, h, 1, far).wait_send())
                pl.when(has_down)(lambda: z_copy(kind, h, 0, far).wait_send())

    pl.loop(1, NX * NZ)(lambda d: c1_copy(d).wait_send())
    for d in range(1, NL):
        l_copy(d).wait_send()
    for d in range(1, NY):
        y_copy(d).wait_send()
    core_copy(core).wait_send()


def local(queries, target_keys, target_values, cond_keys, cond_values):
    rows = queries.shape[1] * NX * NZ
    tables = [t.reshape(-1, HD) for t in trig_tables(rows, COLS)] + [swap_matrix()]
    tables = np.concatenate(tables)
    hbm = pl.BlockSpec(memory_space=pltpu.HBM)
    heads = HG * NX
    dma = pltpu.SemaphoreType.DMA
    return pl.pallas_call(
        kernel,
        out_shape=jax.ShapeDtypeStruct(queries.shape, BF16),
        in_specs=[hbm] * 6,
        out_specs=hbm,
        scratch_shapes=[
            pltpu.VMEM(tables.shape, F32),
            pltpu.VMEM((HD, HD), BF16),
            pltpu.VMEM((1, heads * HD), BF16),
            pltpu.VMEM((1, heads * HD), BF16),
            pltpu.VMEM((RD, COLS, heads * HD), BF16),
            pltpu.VMEM((RD, COLS, heads * HD), BF16),
            pltpu.VMEM((NX, HG, RD, COLS, HD), BF16),
            pltpu.VMEM((NX, HG, RD, COLS, HD), BF16),
            pltpu.VMEM((HG, BR, COLS, HD), BF16),
            pltpu.VMEM((HG, BR, COLS, HD), BF16),
            pltpu.VMEM((HG, LR, COLS, HD), BF16),
            pltpu.VMEM((HG, LR, COLS, HD), BF16),
            pltpu.VMEM((LR, COLS, HD), BF16),
            pltpu.VMEM((BR, COLS, HD), BF16),
            pltpu.VMEM((2, RD * COLS, HD), F32),
            pltpu.VMEM((8 * NX, HD), F32),
            pltpu.VMEM((8 * NX * NZ, HD), F32),
            pltpu.VMEM((2 * HG, CT, HD), BF16),
            dma((5,)),
            dma((4, HG, NX)),
            dma((4, HG, NX)),
            dma((4, 2, HG)),
            dma((4, 2, HG)),
            dma((NX * NZ,)),
            dma((NX * NZ,)),
            dma((NL,)),
            dma((NL,)),
            dma((NY,)),
            dma((NY,)),
            dma((1,)),
            dma((1,)),
        ],
        compiler_params=pltpu.CompilerParams(
            collective_id=0, has_side_effects=True, vmem_limit_bytes=60 * 1024 * 1024
        ),
        cost_estimate=pl.CostEstimate(flops=8_000_000_000, bytes_accessed=5_000_000, transcendentals=8_000_000),
    )(
        queries, target_keys, target_values, cond_keys, cond_values, jnp.asarray(tables)
    )


def solution(mesh):
    return jax.shard_map(
        local,
        mesh=mesh,
        in_specs=(
            P("view", "row", None, None),
            P("view", "row", None, None),
            P("view", "row", None, None),
            P(("view", "row"), None),
            P(("view", "row"), None),
        ),
        out_specs=P("view", "row", None, None),
        check_vma=False,
    )
```

```python
import functools
import math

import jax
import jax.numpy as jnp
import numpy as np
from jax import lax
from jax.experimental import pallas as pl
from jax.experimental.pallas import tpu as pltpu
from jax.sharding import PartitionSpec as P

HD = 128
RADIUS = 8
BASE = 10000.0
BIG = 1e30
COLS = 64
NX = 4
NZ = 4
NL = 4
NY = 4
RD = 4
HG = 4
LR = RD * NX
BR = LR + 2 * RADIUS
CT = 512
ROWS = LR * NZ
VIEW_ROWS = 40
VIEW_TAB, ROW_TAB, COL_TAB, SWAP_TAB = 0, 2 * VIEW_ROWS, 2 * (VIEW_ROWS + ROWS), 2 * (VIEW_ROWS + ROWS + COLS)
V, K, Q, O = range(4)
F32 = jnp.float32
BF16 = jnp.bfloat16


def trig_tables(rows, cols):
    widths = (HD // 4, 3 * HD // 8, 3 * HD // 8)
    counts = (VIEW_ROWS, rows, cols)
    tables, offset = [], 0
    for width, count in zip(widths, counts):
        half = width // 2
        freq = np.power(np.float32(BASE), -np.arange(half, dtype=np.float32) / np.float32(half)).astype(np.float32)
        angle = (np.arange(count, dtype=np.float32)[:, None] * freq).astype(np.float64)
        table = np.zeros((2, count, HD), np.float32)
        for i, f in enumerate((np.cos, np.sin)):
            table[i, :, offset : offset + half] = f(angle)
            table[i, :, offset + half : offset + width] = f(angle)
        tables.append(table)
        offset += width
    return tables


def swap_matrix():
    swap, offset = np.zeros((HD, HD), np.float32), 0
    for width in (HD // 4, 3 * HD // 8, 3 * HD // 8):
        half = width // 2
        for i in range(offset, offset + half):
            swap[i + half, i] = -1.0
            swap[i, i + half] = 1.0
        offset += width
    return swap


def kernel(
    q_hbm, k_hbm, v_hbm, ck_hbm, cv_hbm, tab_hbm, out_hbm,
    tab, swap, ck_ref, cv_ref, kin, qin, kst, qst, k_buf, v_buf, q_buf, o_buf, qaug, kaug, cs, cst, c1, ckv,
    lsem, xs, xr, zs, zr, c1s, c1r, ls, lr, ys, yr, ks, kr,
):
    row = lax.axis_index("row")
    view = lax.axis_index("view")
    x, zh = row % NX, row // NX
    core, zl, y = view % 2, (view // 2) % NL, view // (2 * NL)

    def row_dev(zz, xx):
        return {"view": view, "row": zz * NX + xx}

    def view_dev(yy, ll, cc):
        return {"view": (yy * NL + ll) * 2 + cc, "row": row}

    def remote(src, dst, s, r, dev):
        return pltpu.make_async_remote_copy(
            src_ref=src, dst_ref=dst, send_sem=s, recv_sem=r, device_id=dev, device_id_type=pl.DeviceIdType.MESH
        )

    barrier = pltpu.get_barrier_semaphore()

    def greet(dev):
        pl.semaphore_signal(barrier, inc=1, device_id=dev, device_id_type=pl.DeviceIdType.MESH)

    @pl.loop(1, NX * NZ)
    def _(d):
        greet({"view": view, "row": (row + d) % (NX * NZ)})

    for d in range(1, NL):
        greet(view_dev(y, (zl + d) % NL, core))
    for d in range(1, NY):
        greet(view_dev((y + d) % NY, zl, core))
    greet(view_dev(y, zl, 1 - core))

    loads = [
        pltpu.make_async_copy(src, dst, lsem.at[i])
        for i, (src, dst) in enumerate(
            ((tab_hbm, tab), (ck_hbm, ck_ref), (cv_hbm, cv_ref), (k_hbm.at[0], kin), (q_hbm.at[0], qin))
        )
    ]
    for load in loads:
        load.start()


    def own_rows(buf, h, xx):
        return buf.at[h, pl.ds(RADIUS + RD * xx, RD)]

    def x_src(kind, h, p):
        if kind == V:
            return v_hbm.at[0, :, :, pl.ds(pl.multiple_of((HG * p + h) * HD, HD), HD)]
        return (kst if kind == K else qst).at[p, h]

    def x_dst(kind, h, xx):
        if kind == Q:
            return q_buf.at[h, pl.ds(RD * xx, RD)]
        return own_rows(k_buf if kind == K else v_buf, h, xx)

    def x_copy(kind, h, d):
        p = (x + d) % NX
        return remote(x_src(kind, h, p), x_dst(kind, h, x), xs.at[kind, h, p], xr.at[kind, h, x], row_dev(zh, p))

    def x_own(kind, h):
        return pltpu.make_async_copy(x_src(kind, h, x), x_dst(kind, h, x), xs.at[kind, h, x])

    def x_send(kind, h):
        for d in (2, 1, 3):
            x_copy(kind, h, d).start()
        x_own(kind, h).start()

    def x_from(kind, h, p):
        @pl.when(p != x)
        def _():
            remote(x_src(kind, h, x), x_dst(kind, h, p), xs.at[kind, h, x], xr.at[kind, h, p], row_dev(zh, p)).wait_recv()

        @pl.when(p == x)
        def _():
            x_own(kind, h).wait()

    def rope(src, dst, h):
        @pl.loop(0, NX)
        def _(p):
            feats = src[:, :, pl.ds(pl.multiple_of((HG * p + h) * HD, HD), HD)].reshape(RD * COLS, HD)
            turned = jnp.dot(feats, swap[...], preferred_element_type=F32)
            out = feats.astype(F32) * cs[0] + turned * cs[1]
            dst[p, h] = out.astype(BF16).reshape(RD, COLS, HD)

    def z_copy(kind, h, up, far):
        buf = k_buf if kind == K else v_buf
        if up:
            src, dst = RADIUS + LR - RD * (1 + far), RD * (1 - far)
        else:
            src, dst = RADIUS + RD * far, RADIUS + LR + RD * far
        i = 2 * up + far
        return remote(
            buf.at[h, pl.ds(src, RD)], buf.at[h, pl.ds(dst, RD)],
            zs.at[i, kind, h], zr.at[i, kind, h], row_dev(zh + (1 if up else -1), x),
        )

    has_up, has_down = zh < NZ - 1, zh > 0

    def forward(kind, h):
        for far in (0, 1):
            x_from(kind, h, NX - 1 - far)
            pl.when(has_up)(lambda: z_copy(kind, h, 1, far).start())
            x_from(kind, h, far)
            pl.when(has_down)(lambda: z_copy(kind, h, 0, far).start())

    def c1_copy(d):
        peer = (row + d) % (NX * NZ)
        return remote(
            cst.at[pl.ds(pl.multiple_of((peer % NX) * 8, 8), 8), :],
            c1.at[pl.ds(pl.multiple_of(row * 8, 8), 8), :],
            c1s.at[peer], c1r.at[row], {"view": view, "row": peer},
        )

    def c1_wait(d):
        peer = (row + d) % (NX * NZ)
        remote(
            cst.at[pl.ds(0, 8), :],
            c1.at[pl.ds(pl.multiple_of(peer * 8, 8), 8), :],
            c1s.at[peer], c1r.at[peer], {"view": view, "row": peer},
        ).wait_recv()

    def slot(yy, ll, cc, blocks):
        return ckv.at[:, pl.ds(pl.multiple_of(((cc * NY + yy) * NL + ll) * 16, 16), blocks * 16), :]

    def l_copy(d):
        peer = (zl + d) % NL
        return remote(slot(y, zl, core, 1), slot(y, zl, core, 1), ls.at[peer], lr.at[zl], view_dev(y, peer, core))

    def l_wait(d):
        peer = (zl + d) % NL
        remote(slot(y, zl, core, 1), slot(y, peer, core, 1), ls.at[peer], lr.at[peer], view_dev(y, peer, core)).wait_recv()

    def y_copy(d):
        peer = (y + d) % NY
        return remote(slot(y, 0, core, NL), slot(y, 0, core, NL), ys.at[peer], yr.at[y], view_dev(peer, zl, core))

    def y_wait(d):
        peer = (y + d) % NY
        remote(slot(y, 0, core, NL), slot(peer, 0, core, NL), ys.at[peer], yr.at[peer], view_dev(peer, zl, core)).wait_recv()

    def core_copy(cc):
        return remote(slot(0, 0, cc, NL * NY), slot(0, 0, cc, NL * NY), ks.at[0], kr.at[0], view_dev(y, zl, 1 - core))

    for load in loads[:3]:
        load.wait()
    swap[...] = tab[pl.ds(SWAP_TAB, HD), :].astype(BF16)

    for i in range(2):
        base = tab[pl.ds(COL_TAB + i * COLS, COLS), :] + tab[pl.ds(VIEW_TAB + i * VIEW_ROWS + view + 1, 1), :]
        for r in range(RD):
            cs[i, pl.ds(r * COLS, COLS), :] = base + tab[pl.ds(ROW_TAB + i * ROWS + row * RD + r, 1), :]

    for h in range(HG * NX):
        p, hh = h // HG, h % HG
        cst[pl.ds(p * 8 + hh, 1), :] = ck_ref[:, pl.ds(h * HD, HD)].astype(F32)
        cst[pl.ds(p * 8 + HG + hh, 1), :] = cv_ref[:, pl.ds(h * HD, HD)].astype(F32)
    token = view * (NX * NZ) + row
    ctok = [
        tab[pl.ds(VIEW_TAB + i * VIEW_ROWS, 1), :]
        + tab[pl.ds(ROW_TAB + i * ROWS + token // COLS, 1), :]
        + tab[pl.ds(COL_TAB + i * COLS + token % COLS, 1), :]
        for i in range(2)
    ]
    ckin = cst[...]
    crot = jnp.dot(ckin.astype(BF16), swap[...], preferred_element_type=F32)
    crot = (ckin * ctok[0] + crot * ctok[1]).astype(BF16).astype(F32)
    is_key = lax.broadcasted_iota(jnp.int32, (8 * NX, HD), 0) % 8 < HG
    cst[...] = jnp.where(is_key, crot, ckin)
    c1[pl.ds(pl.multiple_of(row * 8, 8), 8), :] = cst[pl.ds(pl.multiple_of(x * 8, 8), 8), :]

    for edge, first in ((0, 0), (NZ - 1, RADIUS + LR)):

        @pl.when(zh == edge)
        def _():
            @pl.loop(0, HG)
            def _(h):
                @pl.loop(0, RADIUS)
                def _(r):
                    k_buf[h, first + r] = jnp.zeros((COLS, HD), BF16)
                    v_buf[h, first + r] = jnp.zeros((COLS, HD), BF16)

    loads[3].wait()
    rope(kin, kst, 0)
    rope(kin, kst, 1)

    pl.semaphore_wait(barrier, NX * NZ - 1 + NL - 1 + NY - 1 + 1)
    x_send(V, 0)
    pl.loop(1, NX * NZ)(lambda d: c1_copy(d).start())
    forward(V, 0)
    x_send(K, 0)
    forward(K, 0)
    x_send(V, 1)
    x_send(K, 1)
    pl.loop(1, NX * NZ)(c1_wait)
    for i in range(8):
        rows16 = c1[pl.ds(i, NX * NZ, stride=8), :]
        ckv[i, pl.ds(pl.multiple_of(((core * NY + y) * NL + zl) * 16, 16), 16), :] = rows16.astype(BF16)
    for d in range(1, NL):
        l_copy(d).start()
    x_send(V, 2)
    rope(kin, kst, 2)
    x_send(K, 2)
    forward(V, 1)
    forward(K, 1)
    x_send(V, 3)
    rope(kin, kst, 3)
    x_send(K, 3)
    forward(V, 2)
    loads[4].wait()
    for h in range(HG):
        rope(qin, qst, h)
        x_send(Q, h)
    forward(K, 2)
    forward(V, 3)
    forward(K, 3)

    @pl.loop(0, LR)
    def _(r):
        lane = lax.broadcasted_iota(jnp.int32, (COLS, HD), 1)
        col = lax.broadcasted_iota(jnp.int32, (COLS, HD), 0)
        low = jnp.where(zh == 0, 80, -1)
        high = jnp.where(zh == NZ - 1, 81, -1)
        on = (lane == col) | (lane == r + COLS) | (lane == low) | (lane == high)
        qaug[r] = jnp.where(on, 1.0, 0.0).astype(BF16)

    @pl.loop(0, BR)
    def _(r):
        lane = lax.broadcasted_iota(jnp.int32, (COLS, HD), 1)
        col = lax.broadcasted_iota(jnp.int32, (COLS, HD), 0)
        low = jnp.where(r < RADIUS, 80, -1)
        high = jnp.where(r >= RADIUS + LR, 81, -1)
        far_col = (lane < COLS) & (jnp.abs(lane - col) > RADIUS)
        apart = r - (lane - COLS)
        far_row = (lane >= COLS) & (lane < COLS + LR) & ((apart < 0) | (apart > 2 * RADIUS))
        off = far_col | far_row | (lane == low) | (lane == high)
        kaug[r] = jnp.where(off, -BIG, 0.0).astype(BF16)

    for d in range(1, NL):
        l_wait(d)
    for d in range(1, NY):
        y_copy(d).start()
    for d in range(1, NY):
        y_wait(d)
    core_copy(core).start()
    core_copy(1 - core).wait_recv()

    def o_copy(h, b):
        return remote(
            o_buf.at[h, pl.ds(RD * b, RD)],
            out_hbm.at[0, :, :, pl.ds(pl.multiple_of((HG * x + h) * HD, HD), HD)],
            xs.at[O, h, b], xr.at[O, h, x], row_dev(zh, b),
        )

    def o_own(h):
        return pltpu.make_async_copy(
            o_buf.at[h, pl.ds(RD * x, RD)],
            out_hbm.at[0, :, :, pl.ds(pl.multiple_of((HG * x + h) * HD, HD), HD)],
            xs.at[O, h, x],
        )

    def o_wait(h, p):
        remote(
            o_buf.at[h, pl.ds(RD * p, RD)],
            out_hbm.at[0, :, :, pl.ds(pl.multiple_of((HG * p + h) * HD, HD), HD)],
            xs.at[O, h, p], xr.at[O, h, p], row_dev(zh, p),
        ).wait_recv()

    scale = math.log2(math.e) / math.sqrt(HD)
    nt = (((1,), (1,)), ((), ()))

    def block(h, b):
        n, band = RD * COLS, (RD + 2 * RADIUS) * COLS
        qb = q_buf[h, pl.ds(RD * b, RD)].reshape(n, HD)
        qa = qaug[pl.ds(RD * b, RD)].reshape(n, HD)
        kb = k_buf[h, pl.ds(RD * b, RD + 2 * RADIUS)].reshape(band, HD)
        ka = kaug[pl.ds(RD * b, RD + 2 * RADIUS)].reshape(band, HD)
        s1 = lax.dot_general(
            jnp.concatenate([qb, qa], axis=1), jnp.concatenate([kb, ka], axis=1), nt, preferred_element_type=F32
        )
        s2 = lax.dot_general(qb, ckv[h], nt, preferred_element_type=F32)
        m = jnp.maximum(jnp.max(s1, axis=1, keepdims=True), jnp.max(s2, axis=1, keepdims=True))
        p1 = jnp.exp2((s1 - m) * scale).astype(BF16)
        p2 = jnp.exp2((s2 - m) * scale).astype(BF16)
        vb = v_buf[h, pl.ds(RD * b, RD + 2 * RADIUS)].reshape(band, HD)
        acc = jnp.dot(p1, jnp.concatenate([vb, jnp.ones((band, HD), BF16)], axis=1), preferred_element_type=F32)
        acc += jnp.dot(
            p2, jnp.concatenate([ckv[HG + h], jnp.ones((CT, HD), BF16)], axis=1), preferred_element_type=F32
        )
        o_buf[h, pl.ds(RD * b, RD)] = (acc[:, :HD] / acc[:, HD:]).astype(BF16).reshape(RD, COLS, HD)

    @pl.loop(0, HG)
    def _(h):
        for p in range(NX):
            x_from(Q, h, p)
        for b in (1, 2, 0, 3):
            up, far = b < NX // 2, b in (0, NX - 1)
            for kind in (V, K):
                pl.when(has_down if up else has_up)(lambda: z_copy(kind, h, up, far).wait_recv())
            block(h, b)
            pl.when(x != b)(lambda: o_copy(h, b).start())
            pl.when(x == b)(lambda: o_own(h).start())

    @pl.loop(0, HG)
    def _(h):
        for d in range(1, NX):
            p = (x + d) % NX
            o_wait(h, p)
            o_copy(h, p).wait_send()
            for kind in (V, K, Q):
                x_copy(kind, h, d).wait_send()
        o_own(h).wait()
        for kind in (V, K):
            for far in (0, 1):
                pl.when(has_up)(lambda: z_copy(kind, h, 1, far).wait_send())
                pl.when(has_down)(lambda: z_copy(kind, h, 0, far).wait_send())

    pl.loop(1, NX * NZ)(lambda d: c1_copy(d).wait_send())
    for d in range(1, NL):
        l_copy(d).wait_send()
    for d in range(1, NY):
        y_copy(d).wait_send()
    core_copy(core).wait_send()


def local(queries, target_keys, target_values, cond_keys, cond_values):
    rows = queries.shape[1] * NX * NZ
    tables = [t.reshape(-1, HD) for t in trig_tables(rows, COLS)] + [swap_matrix()]
    tables = np.concatenate(tables)
    hbm = pl.BlockSpec(memory_space=pltpu.HBM)
    heads = HG * NX
    dma = pltpu.SemaphoreType.DMA
    return pl.pallas_call(
        kernel,
        out_shape=jax.ShapeDtypeStruct(queries.shape, BF16),
        in_specs=[hbm] * 6,
        out_specs=hbm,
        scratch_shapes=[
            pltpu.VMEM(tables.shape, F32),
            pltpu.VMEM((HD, HD), BF16),
            pltpu.VMEM((1, heads * HD), BF16),
            pltpu.VMEM((1, heads * HD), BF16),
            pltpu.VMEM((RD, COLS, heads * HD), BF16),
            pltpu.VMEM((RD, COLS, heads * HD), BF16),
            pltpu.VMEM((NX, HG, RD, COLS, HD), BF16),
            pltpu.VMEM((NX, HG, RD, COLS, HD), BF16),
            pltpu.VMEM((HG, BR, COLS, HD), BF16),
            pltpu.VMEM((HG, BR, COLS, HD), BF16),
            pltpu.VMEM((HG, LR, COLS, HD), BF16),
            pltpu.VMEM((HG, LR, COLS, HD), BF16),
            pltpu.VMEM((LR, COLS, HD), BF16),
            pltpu.VMEM((BR, COLS, HD), BF16),
            pltpu.VMEM((2, RD * COLS, HD), F32),
            pltpu.VMEM((8 * NX, HD), F32),
            pltpu.VMEM((8 * NX * NZ, HD), F32),
            pltpu.VMEM((2 * HG, CT, HD), BF16),
            dma((5,)),
            dma((4, HG, NX)),
            dma((4, HG, NX)),
            dma((4, 2, HG)),
            dma((4, 2, HG)),
            dma((NX * NZ,)),
            dma((NX * NZ,)),
            dma((NL,)),
            dma((NL,)),
            dma((NY,)),
            dma((NY,)),
            dma((1,)),
            dma((1,)),
        ],
        compiler_params=pltpu.CompilerParams(
            collective_id=0, has_side_effects=True, vmem_limit_bytes=60 * 1024 * 1024
        ),
        cost_estimate=pl.CostEstimate(flops=8_000_000_000, bytes_accessed=5_000_000, transcendentals=8_000_000),
    )(
        queries, target_keys, target_values, cond_keys, cond_values, jnp.asarray(tables)
    )


def solution(mesh):
    return jax.shard_map(
        local,
        mesh=mesh,
        in_specs=(
            P("view", "row", None, None),
            P("view", "row", None, None),
            P("view", "row", None, None),
            P(("view", "row"), None),
            P(("view", "row"), None),
        ),
        out_specs=P("view", "row", None, None),
        check_vma=False,
    )
```
